32 devices in a mesh: group: 2 (over x), feat: 16 (over z, y, core).
Axes of the slice: x: 2, y: 2, z: 4, core: 2. Of those that a mesh axis runs over, the one named last changes fastest.
Arguments:
- hidden: bfloat16 [8192, 14336], P('group', 'feat'), parts along dimension 0, may hold values from -8 to 8
- grad_out: bfloat16 [8192, 4096], P('group', 'feat'), parts along dimension 0, may hold values from -8 to 8
- proj_in: bfloat16 [14336, 128], P('feat'), may hold values from -0.046875 to 0.046875
- proj_out: bfloat16 [4096, 128], P('feat'), may hold values from -0.09375 to 0.09375
- inv_out: float32 [128, 128], replicated, may hold values from -0.5 to 0.5
- inv_in: float32 [128, 128], replicated, may hold values from -0.5 to 0.5
- queries: bfloat16 [8192, 16384], P(None, 'feat'), may hold values from -0.01171875 to 0.01171875
Outputs:
- scores: float32 [8192, 256], P('feat', 'group'), parts along dimension 1
The draws below stay inside these ranges and needn't reach their ends.
There are 2 independent parts, one for each index of `group`. The reference program is written for one: setup_inputs(seed, part) draws one part's arguments, and reference() takes and returns one part's arrays. A program takes and returns all parts, laid end to end along the dimension named above; an argument that names none is the same for every part. Nothing has to cross between parts.
All inputs are finite; a program needn't handle non-finite values.
Results may differ from the reference program's by a relative error of at most 0.005.
Values may be sent and summed in bfloat16 or wider, within the bound.
A program may use at most 64 MiB of HBM per device.

```python
import jax
import jax.numpy as jnp
from jax import lax

D = 4096
FF = 14336
R = 128
L = 32
EX = 128
NQ = 8192
TOK = 4096
FEATS = 16384


def strengthened(result, own_key, source, target, blocks, factor):
    def block_of(dim):
        return (jnp.arange(result.shape[dim]) // (result.shape[dim] // blocks)).reshape((-1,) + (1,) * (result.ndim - 1 - dim))

    first = jax.random.permutation(own_key, blocks)[block_of(target)]
    far = (block_of(target) + blocks // 2) % blocks
    return jnp.where((block_of(source) == first) | (block_of(source) == far), factor * result, result)


def level_of(stream_key, shape, shards, low, top_value):
    factor_of = 1.0
    for position, blocks in shards:
        heights = jax.random.uniform(jax.random.fold_in(jax.random.fold_in(stream_key, 6), position), (blocks,), jnp.float32, low / len(shards), top_value / len(shards))
        factor_of = factor_of * jnp.repeat(jnp.exp(heights), shape[position] // blocks).reshape((-1,) + (1,) * (len(shape) - 1 - position))
    return factor_of


def gaussian(stream_key, dims, scale, bound, split=(), held_as=jnp.bfloat16):
    entries = scale * jax.random.normal(stream_key, dims, jnp.float32)
    if split:
        entries = entries * level_of(stream_key, dims, split, -0.22, 0.18)
    return jnp.clip(entries, -bound, bound).astype(held_as)


def heavy_noise(key, dims, deviation, bound, shards, heavy, dtype=jnp.bfloat16):
    entries = deviation * jax.random.normal(key, dims, jnp.float32)
    if shards:
        entries = entries * level_of(key, dims, shards, -0.22, 0.18)
    return jnp.clip(strengthened(entries, jax.random.fold_in(key, 3), *heavy), -bound, bound).astype(dtype)


def setup_inputs(seed: int = 0, part: int = 0) -> dict:
    keys = jax.random.split(jax.random.key(seed), 8)
    own_keys = jax.random.split(jax.random.fold_in(keys[7], part), 8)
    return {
        "hidden": heavy_noise(own_keys[0], (TOK, FF), 1.0, 8.0, ((1, 16),), (1, 0, 16, 2.0)),
        "grad_out": heavy_noise(own_keys[1], (TOK, D), 1.0, 8.0, ((1, 16),), (1, 0, 16, 2.0)),
        "proj_in": gaussian(keys[2], (FF, R), FF ** -0.5, 0.046875, ((0, 16),)),
        "proj_out": gaussian(keys[3], (D, R), D ** -0.5, 0.09375, ((0, 16),)),
        "inv_out": gaussian(keys[4], (R, R), R ** -0.5, 0.5, (), jnp.float32),
        "inv_in": gaussian(keys[5], (R, R), R ** -0.5, 0.5, (), jnp.float32),
        "queries": heavy_noise(keys[6], (NQ, FEATS), (1.0 / (R * 6.0)), 0.01171875, ((1, 16),), (1, 0, 16, 2.0)),
    }


def reference(hidden, grad_out, proj_in, proj_out, inv_out, inv_in, queries):
    in_low = jnp.dot(hidden, proj_in, preferred_element_type=jnp.float32).astype(jnp.bfloat16)
    out_low = jnp.dot(grad_out, proj_out, preferred_element_type=jnp.float32).astype(jnp.bfloat16)
    in_seq = in_low.astype(jnp.float32).reshape(EX, L, R)
    out_seq = out_low.astype(jnp.float32).reshape(EX, L, R)
    per_example = jnp.einsum("elo,eli->eoi", out_seq, in_seq)
    left = jnp.einsum("po,eoi->epi", inv_out, per_example, precision=lax.Precision.HIGHEST)
    conditioned = jnp.einsum("epi,iq->epq", left, inv_in, precision=lax.Precision.HIGHEST)
    conditioned = conditioned.reshape(EX, R * R).astype(jnp.bfloat16)
    return lax.dot_general(queries, conditioned, (((1,), (1,)), ((), ())), preferred_element_type=jnp.float32)
```

```python
import functools

import jax
import jax.numpy as jnp
from jax import lax
from jax.experimental import pallas as pl
from jax.experimental.pallas import tpu as pltpu
from jax.sharding import PartitionSpec as P

L = 32
LANES = 128
SCALE = 2.0 ** 48
F32 = jnp.float32
BF16 = jnp.bfloat16
EXACT = lax.Precision.HIGHEST


def plain(hidden, grad_out, proj_in, proj_out, inv_out, inv_in, queries):
    count_dev = lax.axis_size("feat")
    tok_rows = hidden.shape[0] // count_dev
    rank = proj_in.shape[1]
    in_part = jnp.dot(hidden, proj_in, preferred_element_type=F32)
    out_part = jnp.dot(grad_out, proj_out, preferred_element_type=F32)
    low_rows = lax.psum_scatter(
        jnp.concatenate([in_part, out_part], axis=1), "feat", scatter_dimension=0, tiled=True
    )
    in_low = low_rows[:, :rank].astype(BF16)
    out_low = low_rows[:, rank:].astype(BF16)
    seq_count = tok_rows // L
    in_seq = in_low.reshape(seq_count, L, rank)
    out_seq = out_low.reshape(seq_count, L, rank)
    per_example = jnp.einsum("elo,eli->eoi", out_seq, in_seq, preferred_element_type=F32)
    left = jnp.einsum("po,eoi->epi", inv_out, per_example, precision=EXACT)
    conditioned = jnp.einsum("epi,iq->epq", left, inv_in, precision=EXACT)
    conditioned = conditioned.reshape(seq_count, rank * rank).astype(BF16)
    contract = (((1,), (1,)), ((), ()))
    tiles = lax.all_to_all(conditioned, "feat", split_axis=1, concat_axis=0, tiled=True)
    return lax.psum_scatter(
        lax.dot_general(queries, tiles, contract, preferred_element_type=F32),
        "feat",
        scatter_dimension=0,
        tiled=True,
    )


def code_square(x):
    x = x * SCALE
    return (x * jnp.abs(x)).astype(BF16)


def decode_square(y):
    y = y.astype(F32)
    root = jnp.sqrt(jnp.abs(y)) * (1.0 / SCALE)
    return jnp.where(y < 0, -root, root)


def code_plain(x):
    return x.astype(BF16)


def decode_plain(y):
    return y.astype(F32)


class Scatter:
    def __init__(self, n, me, rows, bufs, sems, code, decode, product):
        self.steps = n // 4
        self.c, self.b, self.a = me % 2, (me // 2) % 2, me // 4
        self.me, self.rows = me, rows
        self.own, self.csend, self.crecv, self.ysend, self.yrecv, self.zsend, self.zrecv = bufs
        self.sems = sems
        self.code, self.decode, self.product = code, decode, product

    def target(self, t):
        return (self.a + 1 + t) % self.steps

    def copy(self, stage, t, src, dst, to):
        return pltpu.make_async_remote_copy(
            src_ref=src.at[t], dst_ref=dst.at[t],
            send_sem=self.sems.at[stage, 0, t], recv_sem=self.sems.at[stage, 1, t],
            device_id={"feat": to}, device_id_type=pl.DeviceIdType.MESH,
        )

    def core(self, t):
        return self.copy(0, t, self.csend, self.crecv, self.me + 1 - 2 * self.c)

    def side(self, t):
        return self.copy(1, t, self.ysend, self.yrecv, self.me + 2 - 4 * self.b)

    def far(self, t):
        return self.copy(2, t, self.zsend, self.zrecv, self.target(t) * 4 + self.me % 4)

    def compute_send(self, t):
        for b in range(2):
            self.csend[t, b] = self.product((self.target(t) * 2 + b) * 2 + 1 - self.c).astype(self.csend.dtype)

    def compute_own(self, t):
        for b in range(2):
            self.own[t, b] = self.product((self.target(t) * 2 + b) * 2 + self.c)

    def stage_y(self, t):
        self.core(t).wait_recv()
        other = 1 - self.b
        self.ysend[t] = self.code(self.own[t, other] + self.crecv[t, other].astype(F32))
        self.side(t).start()

    def held(self, t):
        self.side(t).wait_recv()
        return self.own[t, self.b] + self.crecv[t, self.b].astype(F32) + self.decode(self.yrecv[t])

    def stage_z(self, t):
        self.zsend[t] = self.code(self.held(t))
        self.far(t).start()

    def run(self, ready, entered):
        last = self.steps - 1
        for i in range(self.steps + 2):
            if i < self.steps:
                ready(i)
                self.compute_send(i)
                if i == 0:
                    entered()
                self.core(i).start()
                self.compute_own(i)
            if 0 <= i - 1 < self.steps:
                self.stage_y(i - 1)
            if 0 <= i - 3 < last:
                self.stage_z(i - 3)
        for t in range(max(self.steps - 1, 0), last):
            self.stage_z(t)
        total = self.held(last)
        for t in range(last):
            self.far(t).wait_recv()
            total = total + self.decode(self.zrecv[t])
        return total

    def finish(self):
        for t in range(self.steps):
            self.core(t).wait_send()
            self.side(t).wait_send()
            if t < self.steps - 1:
                self.far(t).wait_send()


def kernel(n, hid_hbm, grad_hbm, pin_ref, pout_ref, iout_ref, iin_ref, que_hbm, out_ref,
           hid, grad, que, low_in, low_out, condf, cond, got, ct,
           own1, cs1, cr1, ys1, yr1, zs1, zr1,
           own2, cs2, cr2, ys2, yr2, zs2, zr2,
           load_sems, sems1, sems2, a2a_sems):
    me = lax.axis_index("feat")
    steps = n // 4
    rank = pin_ref.shape[1]
    tok = hid.shape[0] // n
    seqs = tok // L
    qrows = que.shape[0] // n
    local_p = rank // n

    barrier = pltpu.get_barrier_semaphore()
    for j in range(1, n):
        pl.semaphore_signal(barrier, inc=1, device_id={"feat": (me + j) % n},
                            device_id_type=pl.DeviceIdType.MESH)

    def entered():
        pl.semaphore_wait(barrier, n - 1)

    def project(chunk):
        at = pl.ds(pl.multiple_of(chunk * tok, tok), tok)
        return jnp.concatenate([
            jnp.dot(hid[at, :], pin_ref[...], preferred_element_type=F32),
            jnp.dot(grad[at, :], pout_ref[...], preferred_element_type=F32),
        ], axis=1)

    def score(chunk):
        at = pl.ds(pl.multiple_of(chunk * qrows, qrows), qrows)
        return lax.dot_general(que[at, :], ct[...], (((1,), (1,)), ((), ())), preferred_element_type=F32)

    first = Scatter(n, me, tok, (own1, cs1, cr1, ys1, yr1, zs1, zr1), sems1, code_square, decode_square, project)
    second = Scatter(n, me, qrows, (own2, cs2, cr2, ys2, yr2, zs2, zr2), sems2, code_plain, decode_plain, score)

    def load(hbm, vmem, which, t):
        size = hbm.shape[0] // steps
        at = pl.ds(pl.multiple_of(first.target(t) * size, size), size)
        return pltpu.make_async_copy(hbm.at[at, :], vmem.at[at, :], load_sems.at[which, t])

    for t in range(steps):
        load(hid_hbm, hid, 0, t).start()
        load(grad_hbm, grad, 1, t).start()

    def ready1(t):
        load(hid_hbm, hid, 0, t).wait()
        load(grad_hbm, grad, 1, t).wait()
        if t == steps - 1:
            for s in range(steps):
                load(que_hbm, que, 2, s).start()

    low = first.run(ready1, entered)

    low_in[...] = jnp.dot(low[:, :rank], iin_ref[...], precision=EXACT, preferred_element_type=F32)
    low_out[...] = lax.dot_general(low[:, rank:], iout_ref[...], (((1,), (1,)), ((), ())),
                                   precision=EXACT, preferred_element_type=F32)
    for e in range(seqs):
        at = pl.ds(e * L, L)
        condf[:, e, :] = lax.dot_general(low_out[at, :], low_in[at, :], (((0,), (0,)), ((), ())),
                                         precision=EXACT, preferred_element_type=F32)
    cond[...] = condf[...].reshape(n, local_p * seqs, rank).astype(BF16)

    def tile(j, slot):
        return pltpu.make_async_remote_copy(
            src_ref=cond.at[(me + j) % n], dst_ref=got.at[slot],
            send_sem=a2a_sems.at[0, j], recv_sem=a2a_sems.at[1, j],
            device_id={"feat": (me + j) % n}, device_id_type=pl.DeviceIdType.MESH,
        )

    for j in range(1, n):
        tile(j, me).start()
    got[me] = cond[me]
    for j in range(1, n):
        tile(j, (me + n - j) % n).wait_recv()
    for p in range(local_p):
        parts = got[...].astype(F32).reshape(n, local_p, seqs, rank)[:, p]
        ct[:, p * rank:(p + 1) * rank] = parts.reshape(n * seqs, rank).astype(BF16)

    def ready2(t):
        load(que_hbm, que, 2, t).wait()

    out_ref[...] = second.run(ready2, lambda: None)
    first.finish()
    second.finish()
    for j in range(1, n):
        tile(j, me).wait_send()


def scatter_scratch(steps, rows, cols, core_type):
    far = max(steps - 1, 1)
    return [
        pltpu.VMEM((steps, 2, rows, cols), F32),
        pltpu.VMEM((steps, 2, rows, cols), core_type),
        pltpu.VMEM((steps, 2, rows, cols), core_type),
        pltpu.VMEM((steps, rows, cols), BF16),
        pltpu.VMEM((steps, rows, cols), BF16),
        pltpu.VMEM((far, rows, cols), BF16),
        pltpu.VMEM((far, rows, cols), BF16),
    ]


def on_device(hidden, grad_out, proj_in, proj_out, inv_out, inv_in, queries):
    n = lax.axis_size("feat")
    tokens, rank = hidden.shape[0], proj_in.shape[1]
    tok = tokens // n
    seqs = tok // L
    fits = (
        n % 4 == 0 and n > 4 and rank == LANES and rank % n == 0 and tok % L == 0 and seqs % 8 == 0
        and hidden.shape[1] % LANES == 0 and grad_out.shape[1] % LANES == 0
        and queries.shape[0] % (16 * n) == 0
    )
    if not fits:
        return plain(hidden, grad_out, proj_in, proj_out, inv_out, inv_in, queries)
    steps = n // 4
    local_p = rank // n
    qrows = queries.shape[0] // n
    vmem = pl.BlockSpec(memory_space=pltpu.VMEM)
    hbm = pl.BlockSpec(memory_space=pl.ANY)
    return pl.pallas_call(
        functools.partial(kernel, n),
        out_shape=jax.ShapeDtypeStruct((qrows, n * seqs), F32),
        in_specs=[hbm, hbm, vmem, vmem, vmem, vmem, hbm],
        out_specs=vmem,
        scratch_shapes=[
            pltpu.VMEM(hidden.shape, BF16),
            pltpu.VMEM(grad_out.shape, BF16),
            pltpu.VMEM(queries.shape, BF16),
            pltpu.VMEM((tok, rank), F32),
            pltpu.VMEM((tok, rank), F32),
            pltpu.VMEM((rank, seqs, rank), F32),
            pltpu.VMEM((n, local_p * seqs, rank), BF16),
            pltpu.VMEM((n, local_p * seqs, rank), BF16),
            pltpu.VMEM((n * seqs, local_p * rank), BF16),
            *scatter_scratch(steps, tok, 2 * rank, F32),
            *scatter_scratch(steps, qrows, n * seqs, F32),
            pltpu.SemaphoreType.DMA((3, steps)),
            pltpu.SemaphoreType.DMA((3, 2, steps)),
            pltpu.SemaphoreType.DMA((3, 2, steps)),
            pltpu.SemaphoreType.DMA((2, n)),
        ],
        compiler_params=pltpu.CompilerParams(
            collective_id=0, has_side_effects=True, vmem_limit_bytes=58 * 1024 * 1024,
        ),
    )(hidden, grad_out, proj_in, proj_out, inv_out, inv_in, queries)


def solution(mesh):
    placed = (
        P("group", "feat"),
        P("group", "feat"),
        P("feat", None),
        P("feat", None),
        P(),
        P(),
        P(None, "feat"),
    )
    return jax.shard_map(
        on_device, mesh=mesh, in_specs=placed, out_specs=P("feat", "group"), check_vma=False
    )
```

```python
import functools

import jax
import jax.numpy as jnp
from jax import lax
from jax.experimental import pallas as pl
from jax.experimental.pallas import tpu as pltpu
from jax.sharding import PartitionSpec as P

L = 32
LANES = 128
HALVES = 2
SCALE = 2.0 ** 48
F32 = jnp.float32
BF16 = jnp.bfloat16
EXACT = lax.Precision.HIGHEST


def plain(hidden, grad_out, proj_in, proj_out, inv_out, inv_in, queries):
    count_dev = lax.axis_size("feat")
    tok_rows = hidden.shape[0] // count_dev
    rank = proj_in.shape[1]
    in_part = jnp.dot(hidden, proj_in, preferred_element_type=F32)
    out_part = jnp.dot(grad_out, proj_out, preferred_element_type=F32)
    low_rows = lax.psum_scatter(
        jnp.concatenate([in_part, out_part], axis=1), "feat", scatter_dimension=0, tiled=True
    )
    in_low = low_rows[:, :rank].astype(BF16)
    out_low = low_rows[:, rank:].astype(BF16)
    seq_count = tok_rows // L
    in_seq = in_low.reshape(seq_count, L, rank)
    out_seq = out_low.reshape(seq_count, L, rank)
    per_example = jnp.einsum("elo,eli->eoi", out_seq, in_seq, preferred_element_type=F32)
    left = jnp.einsum("po,eoi->epi", inv_out, per_example, precision=EXACT)
    conditioned = jnp.einsum("epi,iq->epq", left, inv_in, precision=EXACT)
    conditioned = conditioned.reshape(seq_count, rank * rank).astype(BF16)
    contract = (((1,), (1,)), ((), ()))
    tiles = lax.all_to_all(conditioned, "feat", split_axis=1, concat_axis=0, tiled=True)
    return lax.psum_scatter(
        lax.dot_general(queries, tiles, contract, preferred_element_type=F32),
        "feat",
        scatter_dimension=0,
        tiled=True,
    )


def code_square(x):
    x = x * SCALE
    return (x * jnp.abs(x)).astype(BF16)


def decode_square(y):
    y = y.astype(F32)
    root = jnp.sqrt(jnp.abs(y)) * (1.0 / SCALE)
    return jnp.where(y < 0, -root, root)


def code_plain(x):
    return x.astype(BF16)


def decode_plain(y):
    return y.astype(F32)


class Scatter:
    def __init__(self, n, me, rows, bufs, sems, code, decode, product):
        self.steps = n // 4
        self.count = HALVES * self.steps
        self.c, self.b, self.a = me % 2, (me // 2) % 2, me // 4
        self.me, self.rows = me, rows
        self.own, self.csend, self.crecv, self.ysend, self.yrecv, self.zsend, self.zrecv = bufs
        self.sems = sems
        self.code, self.decode, self.product = code, decode, product

    def target(self, t):
        return (self.a + 1 + t) % self.steps

    def copy(self, stage, t, src, dst, to):
        return pltpu.make_async_remote_copy(
            src_ref=src, dst_ref=dst,
            send_sem=self.sems.at[stage, 0, t], recv_sem=self.sems.at[stage, 1, t],
            device_id={"feat": to}, device_id_type=pl.DeviceIdType.MESH,
        )

    def core(self, t, k):
        to = self.me + 1 - 2 * self.c
        return self.copy(k, t, self.csend.at[t, k], self.crecv.at[t, k], to)

    def side(self, t):
        return self.copy(2, t, self.ysend.at[t], self.yrecv.at[t], self.me + 2 - 4 * self.b)

    def far(self, t):
        to = self.target(t % self.steps) * 4 + self.me % 4
        return self.copy(3, t, self.zsend.at[t], self.zrecv.at[t], to)

    def term(self, t, k, c):
        b = self.b if k == 1 else 1 - self.b
        chunk = (self.target(t % self.steps) * 2 + b) * 2 + c
        return self.product(chunk * self.rows + (t // self.steps) * (self.rows // HALVES), self.rows // HALVES)

    def stage_core(self, t, entered):
        for k in range(2):
            self.csend[t, k] = self.term(t, k, 1 - self.c).astype(self.csend.dtype)
            if k == 0:
                entered()
            self.core(t, k).start()
        for k in range(2):
            self.own[t, k] = self.term(t, k, self.c)

    def stage_y(self, t):
        self.core(t, 0).wait_recv()
        self.ysend[t] = self.code(self.own[t, 0] + self.crecv[t, 0].astype(F32))
        self.side(t).start()

    def held(self, t):
        self.core(t, 1).wait_recv()
        self.side(t).wait_recv()
        return self.own[t, 1] + self.crecv[t, 1].astype(F32) + self.decode(self.yrecv[t])

    def stage_z(self, t):
        self.zsend[t] = self.code(self.held(t))
        self.far(t).start()

    def result(self, h):
        base = h * self.steps
        total = self.held(base + self.steps - 1)
        for t in range(base, base + self.steps - 1):
            self.far(t).wait_recv()
            total = total + self.decode(self.zrecv[t])
        return total

    def run(self, ready, entered, done):
        for i in range(self.count + 2):
            if i < self.count:
                if i < self.steps:
                    ready(i)
                self.stage_core(i, entered if i == 0 else lambda: None)
            if 0 <= i - 1 < self.count:
                self.stage_y(i - 1)
            z = i - 3
            if z >= 0 and z % self.steps != self.steps - 1:
                self.stage_z(z)
            if z >= 0 and z % self.steps == 0 and z >= self.steps:
                done(z // self.steps - 1, self.result(z // self.steps - 1))
        done(HALVES - 1, self.result(HALVES - 1))

    def finish(self):
        for t in range(self.count):
            self.core(t, 0).wait_send()
            self.core(t, 1).wait_send()
            self.side(t).wait_send()
            if t % self.steps != self.steps - 1:
                self.far(t).wait_send()


def kernel(n, hid_hbm, grad_hbm, pin_ref, pout_ref, iout_ref, iin_ref, que_hbm, out_ref,
           hid, grad, que, low_in, low_out, condf, cond, got, flat, ct,
           own1, cs1, cr1, ys1, yr1, zs1, zr1,
           own2, cs2, cr2, ys2, yr2, zs2, zr2,
           load_sems, sems1, sems2, a2a_sems):
    me = lax.axis_index("feat")
    steps = n // 4
    rank = pin_ref.shape[1]
    tok = hid.shape[0] // n
    seqs = tok // L
    qrows = que.shape[0] // n
    local_p = rank // n

    barrier = pltpu.get_barrier_semaphore()
    core, side = me + 1 - 2 * (me % 2), me + 2 - 4 * ((me // 2) % 2)
    partners = [core, side] + [(me + 4 * j) % n for j in range(1, steps)]
    for partner in partners:
        pl.semaphore_signal(barrier, inc=1, device_id={"feat": partner},
                            device_id_type=pl.DeviceIdType.MESH)

    def entered():
        pl.semaphore_wait(barrier, len(partners))

    def project(start, size):
        at = pl.ds(pl.multiple_of(start, size), size)
        return jnp.concatenate([
            jnp.dot(hid[at, :], pin_ref[...], preferred_element_type=F32),
            jnp.dot(grad[at, :], pout_ref[...], preferred_element_type=F32),
        ], axis=1)

    def score(start, size):
        at = pl.ds(pl.multiple_of(start, size), size)
        return lax.dot_general(que[at, :], ct[...], (((1,), (1,)), ((), ())), preferred_element_type=F32)

    first = Scatter(n, me, tok, (own1, cs1, cr1, ys1, yr1, zs1, zr1), sems1, code_square, decode_square, project)
    second = Scatter(n, me, qrows, (own2, cs2, cr2, ys2, yr2, zs2, zr2), sems2, code_plain, decode_plain, score)

    def load(hbm, vmem, which, t):
        size = hbm.shape[0] // steps
        at = pl.ds(pl.multiple_of(first.target(t) * size, size), size)
        return pltpu.make_async_copy(hbm.at[at, :], vmem.at[at, :], load_sems.at[which, t])

    for t in range(steps):
        load(hid_hbm, hid, 0, t).start()
        load(grad_hbm, grad, 1, t).start()

    def ready1(t):
        load(hid_hbm, hid, 0, t).wait()
        load(grad_hbm, grad, 1, t).wait()
        if t == steps - 1:
            for s in range(steps):
                load(que_hbm, que, 2, s).start()

    part = seqs // HALVES
    block = part * local_p

    def tile(h, j, slot):
        return pltpu.make_async_remote_copy(
            src_ref=cond.at[h, (me + j) % n], dst_ref=got.at[h, slot],
            send_sem=a2a_sems.at[h, 0, j], recv_sem=a2a_sems.at[h, 1, j],
            device_id={"feat": (me + j) % n}, device_id_type=pl.DeviceIdType.MESH,
        )

    def condition(h, low):
        low_in[...] = jnp.dot(low[:, :rank], iin_ref[...], precision=EXACT, preferred_element_type=F32)
        low_out[...] = lax.dot_general(low[:, rank:], iout_ref[...], (((1,), (1,)), ((), ())),
                                       precision=EXACT, preferred_element_type=F32)
        for e in range(part):
            at = pl.ds(e * L, L)
            one = lax.dot_general(low_out[at, :], low_in[at, :], (((0,), (0,)), ((), ())),
                                  precision=EXACT, preferred_element_type=F32)
            condf[:, e] = one.reshape(n, local_p, rank)
        cond[h] = condf[...].reshape(n, block, rank).astype(BF16)
        for j in range(1, n):
            tile(h, j, me).start()
        got[h, me] = cond[h, me]

    first.run(ready1, entered, condition)

    for h in range(HALVES):
        for j in range(1, n):
            tile(h, j, (me + n - j) % n).wait_recv()
        for s in range(n):
            flat[pl.ds((s * HALVES + h) * block, block), :] = got[h, s].astype(F32)
    for p in range(local_p):
        ct[:, p * rank:(p + 1) * rank] = flat[pl.ds(p, n * seqs, stride=local_p), :].astype(BF16)

    def ready2(t):
        load(que_hbm, que, 2, t).wait()

    def store(h, total):
        out_ref[pl.ds(h * (qrows // HALVES), qrows // HALVES), :] = total

    second.run(ready2, lambda: None, store)
    first.finish()
    second.finish()
    for h in range(HALVES):
        for j in range(1, n):
            tile(h, j, me).wait_send()


def scatter_scratch(steps, rows, cols, core_type):
    count, rows = HALVES * steps, rows // HALVES
    return [
        pltpu.VMEM((count, 2, rows, cols), F32),
        pltpu.VMEM((count, 2, rows, cols), core_type),
        pltpu.VMEM((count, 2, rows, cols), core_type),
        pltpu.VMEM((count, rows, cols), BF16),
        pltpu.VMEM((count, rows, cols), BF16),
        pltpu.VMEM((count, rows, cols), BF16),
        pltpu.VMEM((count, rows, cols), BF16),
    ]


def on_device(hidden, grad_out, proj_in, proj_out, inv_out, inv_in, queries):
    n = lax.axis_size("feat")
    tokens, rank = hidden.shape[0], proj_in.shape[1]
    tok = tokens // n
    seqs = tok // L
    fits = (
        n % 4 == 0 and n > 4 and rank == LANES and rank % n == 0 and tok % L == 0 and seqs % (8 * HALVES // 2) == 0 and (rank // n) % 8 == 0
        and hidden.shape[1] % LANES == 0 and grad_out.shape[1] % LANES == 0
        and queries.shape[0] % (16 * HALVES * n) == 0
    )
    if not fits:
        return plain(hidden, grad_out, proj_in, proj_out, inv_out, inv_in, queries)
    steps = n // 4
    local_p = rank // n
    qrows = queries.shape[0] // n
    vmem = pl.BlockSpec(memory_space=pltpu.VMEM)
    hbm = pl.BlockSpec(memory_space=pl.ANY)
    return pl.pallas_call(
        functools.partial(kernel, n),
        out_shape=jax.ShapeDtypeStruct((qrows, n * seqs), F32),
        in_specs=[hbm, hbm, vmem, vmem, vmem, vmem, hbm],
        out_specs=vmem,
        scratch_shapes=[
            pltpu.VMEM(hidden.shape, BF16),
            pltpu.VMEM(grad_out.shape, BF16),
            pltpu.VMEM(queries.shape, BF16),
            pltpu.VMEM((tok // HALVES, rank), F32),
            pltpu.VMEM((tok // HALVES, rank), F32),
            pltpu.VMEM((n, seqs // HALVES, local_p, rank), F32),
            pltpu.VMEM((HALVES, n, local_p * seqs // HALVES, rank), BF16),
            pltpu.VMEM((HALVES, n, local_p * seqs // HALVES, rank), BF16),
            pltpu.VMEM((n * seqs * local_p, rank), F32),
            pltpu.VMEM((n * seqs, local_p * rank), BF16),
            *scatter_scratch(steps, tok, 2 * rank, F32),
            *scatter_scratch(steps, qrows, n * seqs, F32),
            pltpu.SemaphoreType.DMA((3, steps)),
            pltpu.SemaphoreType.DMA((4, 2, HALVES * steps)),
            pltpu.SemaphoreType.DMA((4, 2, HALVES * steps)),
            pltpu.SemaphoreType.DMA((HALVES, 2, n)),
        ],
        compiler_params=pltpu.CompilerParams(
            collective_id=0, has_side_effects=True, vmem_limit_bytes=58 * 1024 * 1024,
        ),
    )(hidden, grad_out, proj_in, proj_out, inv_out, inv_in, queries)


def solution(mesh):
    placed = (
        P("group", "feat"),
        P("group", "feat"),
        P("feat", None),
        P("feat", None),
        P(),
        P(),
        P(None, "feat"),
    )
    return jax.shard_map(
        on_device, mesh=mesh, in_specs=placed, out_specs=P("feat", "group"), check_vma=False
    )
```

```python
import functools

import jax
import jax.numpy as jnp
from jax import lax
from jax.experimental import pallas as pl
from jax.experimental.pallas import tpu as pltpu
from jax.sharding import PartitionSpec as P

L = 32
LANES = 128
HALVES = 2
SCALE = 2.0 ** 48
F32 = jnp.float32
BF16 = jnp.bfloat16
EXACT = lax.Precision.HIGHEST


def plain(hidden, grad_out, proj_in, proj_out, inv_out, inv_in, queries):
    count_dev = lax.axis_size("feat")
    tok_rows = hidden.shape[0] // count_dev
    rank = proj_in.shape[1]
    in_part = jnp.dot(hidden, proj_in, preferred_element_type=F32)
    out_part = jnp.dot(grad_out, proj_out, preferred_element_type=F32)
    low_rows = lax.psum_scatter(
        jnp.concatenate([in_part, out_part], axis=1), "feat", scatter_dimension=0, tiled=True
    )
    in_low = low_rows[:, :rank].astype(BF16)
    out_low = low_rows[:, rank:].astype(BF16)
    seq_count = tok_rows // L
    in_seq = in_low.reshape(seq_count, L, rank)
    out_seq = out_low.reshape(seq_count, L, rank)
    per_example = jnp.einsum("elo,eli->eoi", out_seq, in_seq, preferred_element_type=F32)
    left = jnp.einsum("po,eoi->epi", inv_out, per_example, precision=EXACT)
    conditioned = jnp.einsum("epi,iq->epq", left, inv_in, precision=EXACT)
    conditioned = conditioned.reshape(seq_count, rank * rank).astype(BF16)
    contract = (((1,), (1,)), ((), ()))
    tiles = lax.all_to_all(conditioned, "feat", split_axis=1, concat_axis=0, tiled=True)
    return lax.psum_scatter(
        lax.dot_general(queries, tiles, contract, preferred_element_type=F32),
        "feat",
        scatter_dimension=0,
        tiled=True,
    )


def code_square(x):
    x = x * SCALE
    return (x * jnp.abs(x)).astype(BF16)


def decode_square(y):
    y = y.astype(F32)
    root = jnp.sqrt(jnp.abs(y)) * (1.0 / SCALE)
    return jnp.where(y < 0, -root, root)


def code_plain(x):
    return x.astype(BF16)


def decode_plain(y):
    return y.astype(F32)


class Scatter:
    def __init__(self, n, me, rows, bufs, sems, code, decode, product):
        self.steps = n // 4
        self.count = HALVES * self.steps
        self.c, self.b, self.a = me % 2, (me // 2) % 2, me // 4
        self.me, self.rows = me, rows
        self.own, self.csend, self.crecv, self.ysend, self.yrecv, self.zsend, self.zrecv = bufs
        self.sems = sems
        self.code, self.decode, self.product = code, decode, product

    def target(self, t):
        return (self.a + 1 + t) % self.steps

    def copy(self, stage, t, src, dst, to):
        return pltpu.make_async_remote_copy(
            src_ref=src, dst_ref=dst,
            send_sem=self.sems.at[stage, 0, t], recv_sem=self.sems.at[stage, 1, t],
            device_id={"feat": to}, device_id_type=pl.DeviceIdType.MESH,
        )

    def core(self, t, k):
        to = self.me + 1 - 2 * self.c
        return self.copy(k, t, self.csend.at[t, k], self.crecv.at[t, k], to)

    def side(self, t):
        return self.copy(2, t, self.ysend.at[t], self.yrecv.at[t], self.me + 2 - 4 * self.b)

    def far(self, t):
        to = self.target(t % self.steps) * 4 + self.me % 4
        return self.copy(3, t, self.zsend.at[t], self.zrecv.at[t], to)

    def term(self, t, k, c):
        b = self.b if k == 1 else 1 - self.b
        chunk = (self.target(t % self.steps) * 2 + b) * 2 + c
        return self.product(chunk * self.rows + (t // self.steps) * (self.rows // HALVES), self.rows // HALVES)

    def stage_core(self, t, entered):
        for k in range(2):
            self.csend[t, k] = self.term(t, k, 1 - self.c).astype(self.csend.dtype)
            if k == 0:
                entered()
            self.core(t, k).start()
        for k in range(2):
            self.own[t, k] = self.term(t, k, self.c)

    def stage_y(self, t):
        self.core(t, 0).wait_recv()
        self.ysend[t] = self.code(self.own[t, 0] + self.crecv[t, 0].astype(F32))
        self.side(t).start()

    def held(self, t):
        self.core(t, 1).wait_recv()
        self.side(t).wait_recv()
        return self.own[t, 1] + self.crecv[t, 1].astype(F32) + self.decode(self.yrecv[t])

    def stage_z(self, t):
        self.zsend[t] = self.code(self.held(t))
        self.far(t).start()

    def result(self, h):
        base = h * self.steps
        total = self.held(base + self.steps - 1)
        for t in range(base, base + self.steps - 1):
            self.far(t).wait_recv()
            total = total + self.decode(self.zrecv[t])
        return total

    def run(self, ready, entered, done):
        for i in range(self.count + 2):
            if i < self.count:
                if i < self.steps:
                    ready(i)
                self.stage_core(i, entered if i == 0 else lambda: None)
            if 0 <= i - 1 < self.count:
                self.stage_y(i - 1)
            z = i - 3
            if z >= 0 and z % self.steps != self.steps - 1:
                self.stage_z(z)
            if z >= 0 and z % self.steps == 0 and z >= self.steps:
                done(z // self.steps - 1, self.result(z // self.steps - 1))
        done(HALVES - 1, self.result(HALVES - 1))

    def finish(self):
        for t in range(self.count):
            self.core(t, 0).wait_send()
            self.core(t, 1).wait_send()
            self.side(t).wait_send()
            if t % self.steps != self.steps - 1:
                self.far(t).wait_send()


def kernel(n, hid_hbm, grad_hbm, pin_ref, pout_ref, iout_ref, iin_ref, que_hbm, out_ref,
           hid, grad, que, low_in, low_out, condf, cond, got, flat, ct,
           own1, cs1, cr1, ys1, yr1, zs1, zr1,
           own2, cs2, cr2, ys2, yr2, zs2, zr2,
           load_sems, sems1, sems2, a2a_sems):
    me = lax.axis_index("feat")
    steps = n // 4
    rank = pin_ref.shape[1]
    tok = hid.shape[0] // n
    seqs = tok // L
    qrows = que.shape[0] // n
    local_p = rank // n

    barrier = pltpu.get_barrier_semaphore()
    core, side = me + 1 - 2 * (me % 2), me + 2 - 4 * ((me // 2) % 2)
    partners = [core, side] + [(me + 4 * j) % n for j in range(1, steps)]
    for partner in partners:
        pl.semaphore_signal(barrier, inc=1, device_id={"feat": partner},
                            device_id_type=pl.DeviceIdType.MESH)

    def entered():
        pl.semaphore_wait(barrier, len(partners))

    def project(start, size):
        at = pl.ds(pl.multiple_of(start, size), size)
        return jnp.concatenate([
            jnp.dot(hid[at, :], pin_ref[...], preferred_element_type=F32),
            jnp.dot(grad[at, :], pout_ref[...], preferred_element_type=F32),
        ], axis=1)

    def score(start, size):
        at = pl.ds(pl.multiple_of(start, size), size)
        return jnp.dot(que[at, :], ct[...], preferred_element_type=F32)

    first = Scatter(n, me, tok, (own1, cs1, cr1, ys1, yr1, zs1, zr1), sems1, code_square, decode_square, project)
    second = Scatter(n, me, qrows, (own2, cs2, cr2, ys2, yr2, zs2, zr2), sems2, code_plain, decode_plain, score)

    def load(hbm, vmem, which, t):
        size = hbm.shape[0] // steps
        at = pl.ds(pl.multiple_of(first.target(t) * size, size), size)
        return pltpu.make_async_copy(hbm.at[at, :], vmem.at[at, :], load_sems.at[which, t])

    for t in range(steps):
        load(hid_hbm, hid, 0, t).start()
        load(grad_hbm, grad, 1, t).start()

    def ready1(t):
        load(hid_hbm, hid, 0, t).wait()
        load(grad_hbm, grad, 1, t).wait()
        if t == steps - 1:
            for s in range(steps):
                load(que_hbm, que, 2, s).start()

    part = seqs // HALVES
    block = part * local_p

    def tile(h, j, slot):
        return pltpu.make_async_remote_copy(
            src_ref=cond.at[h, (me + j) % n], dst_ref=got.at[h, slot],
            send_sem=a2a_sems.at[h, 0, j], recv_sem=a2a_sems.at[h, 1, j],
            device_id={"feat": (me + j) % n}, device_id_type=pl.DeviceIdType.MESH,
        )

    def condition(h, low):
        low_in[...] = jnp.dot(low[:, :rank], iin_ref[...], precision=EXACT, preferred_element_type=F32)
        low_out[...] = lax.dot_general(low[:, rank:], iout_ref[...], (((1,), (1,)), ((), ())),
                                       precision=EXACT, preferred_element_type=F32)
        for e in range(part):
            at = pl.ds(e * L, L)
            one = lax.dot_general(low_out[at, :], low_in[at, :], (((0,), (0,)), ((), ())),
                                  precision=EXACT, preferred_element_type=F32)
            condf[:, e] = one.reshape(n, local_p, rank)
        cond[h] = condf[...].reshape(n, block, rank).astype(BF16)
        for j in range(1, n):
            tile(h, j, me).start()
        got[h, me] = cond[h, me]

    first.run(ready1, entered, condition)

    for h in range(HALVES):
        for j in range(1, n):
            tile(h, j, (me + n - j) % n).wait_recv()
        for s in range(n):
            flat[pl.ds((s * HALVES + h) * block, block), :] = got[h, s].astype(F32)
    for p in range(local_p):
        ct[pl.ds(p * rank, rank), :] = flat[pl.ds(p, n * seqs, stride=local_p), :].T.astype(BF16)

    def ready2(t):
        load(que_hbm, que, 2, t).wait()

    def store(h, total):
        out_ref[pl.ds(h * (qrows // HALVES), qrows // HALVES), :] = total

    second.run(ready2, lambda: None, store)
    first.finish()
    second.finish()
    for h in range(HALVES):
        for j in range(1, n):
            tile(h, j, me).wait_send()


def scatter_scratch(steps, rows, cols, core_type):
    count, rows = HALVES * steps, rows // HALVES
    return [
        pltpu.VMEM((count, 2, rows, cols), F32),
        pltpu.VMEM((count, 2, rows, cols), core_type),
        pltpu.VMEM((count, 2, rows, cols), core_type),
        pltpu.VMEM((count, rows, cols), BF16),
        pltpu.VMEM((count, rows, cols), BF16),
        pltpu.VMEM((count, rows, cols), BF16),
        pltpu.VMEM((count, rows, cols), BF16),
    ]


def on_device(hidden, grad_out, proj_in, proj_out, inv_out, inv_in, queries):
    n = lax.axis_size("feat")
    tokens, rank = hidden.shape[0], proj_in.shape[1]
    tok = tokens // n
    seqs = tok // L
    fits = (
        n % 4 == 0 and n > 4 and rank == LANES and rank % n == 0 and tok % L == 0 and seqs % (8 * HALVES // 2) == 0 and (rank // n) % 8 == 0
        and hidden.shape[1] % LANES == 0 and grad_out.shape[1] % LANES == 0
        and queries.shape[0] % (16 * HALVES * n) == 0
    )
    if not fits:
        return plain(hidden, grad_out, proj_in, proj_out, inv_out, inv_in, queries)
    steps = n // 4
    local_p = rank // n
    qrows = queries.shape[0] // n
    vmem = pl.BlockSpec(memory_space=pltpu.VMEM)
    hbm = pl.BlockSpec(memory_space=pl.ANY)
    return pl.pallas_call(
        functools.partial(kernel, n),
        out_shape=jax.ShapeDtypeStruct((qrows, n * seqs), F32),
        in_specs=[hbm, hbm, vmem, vmem, vmem, vmem, hbm],
        out_specs=vmem,
        scratch_shapes=[
            pltpu.VMEM(hidden.shape, BF16),
            pltpu.VMEM(grad_out.shape, BF16),
            pltpu.VMEM(queries.shape, BF16),
            pltpu.VMEM((tok // HALVES, rank), F32),
            pltpu.VMEM((tok // HALVES, rank), F32),
            pltpu.VMEM((n, seqs // HALVES, local_p, rank), F32),
            pltpu.VMEM((HALVES, n, local_p * seqs // HALVES, rank), BF16),
            pltpu.VMEM((HALVES, n, local_p * seqs // HALVES, rank), BF16),
            pltpu.VMEM((n * seqs * local_p, rank), F32),
            pltpu.VMEM((local_p * rank, n * seqs), BF16),
            *scatter_scratch(steps, tok, 2 * rank, F32),
            *scatter_scratch(steps, qrows, n * seqs, F32),
            pltpu.SemaphoreType.DMA((3, steps)),
            pltpu.SemaphoreType.DMA((4, 2, HALVES * steps)),
            pltpu.SemaphoreType.DMA((4, 2, HALVES * steps)),
            pltpu.SemaphoreType.DMA((HALVES, 2, n)),
        ],
        compiler_params=pltpu.CompilerParams(
            collective_id=0, has_side_effects=True, vmem_limit_bytes=58 * 1024 * 1024,
        ),
    )(hidden, grad_out, proj_in, proj_out, inv_out, inv_in, queries)


def solution(mesh):
    placed = (
        P("group", "feat"),
        P("group", "feat"),
        P("feat", None),
        P("feat", None),
        P(),
        P(),
        P(None, "feat"),
    )
    return jax.shard_map(
        on_device, mesh=mesh, in_specs=placed, out_specs=P("feat", "group"), check_vma=False
    )
```
